32 devices in a mesh: groups: 2 (over y), atoms: 16 (over z, x, core).
Axes of the slice: x: 2, y: 2, z: 4, core: 2. Of those that a mesh axis runs over, the one named last changes fastest.
Arguments:
- xt: bfloat16 [4096, 256], P(None, 'groups'), parts along dimension 1, may hold values from -6 to 6
- dictionary: bfloat16 [16384, 4096], P('atoms'), may hold values from -0.09375 to 0.09375
- dead_index: int32 [32, 32], P(('groups', 'atoms')), parts along dimension 0, may hold values from 0 to 255, as said below
- dead_count: int32 [32], P(('groups', 'atoms')), parts along dimension 0, may hold values from 0 to 32, as said below
- refill_rows: int32 [32, 32], P(('groups', 'atoms')), parts along dimension 0, may hold values from 0 to 127
Outputs:
- codes: bfloat16 [256, 16384], P('groups', 'atoms'), parts along dimension 0
- new_block: bfloat16 [8192, 4096], P(('groups', 'atoms')), parts along dimension 0
- residual: float32 [4096, 256], P('atoms', 'groups'), parts along dimension 1
The draws below stay inside these ranges and needn't reach their ends.
There are 2 independent parts, one for each index of `groups`. The reference program is written for one: setup_inputs(seed, part) draws one part's arguments, and reference() takes and returns one part's arrays. A program takes and returns all parts, laid end to end along the dimension named above; an argument that names none is the same for every part. Nothing has to cross between parts.
Inputs may be any that keep to these rules, and one draw needn't show every extreme that they name: `dead_index`: on each device the 32 entries are distinct positions within its block of 256 atoms. `dead_count`: some device uses all 32 slots.
All inputs are finite; a program needn't handle non-finite values.
Results may differ from the reference program's by a relative error of at most 0.006.
Values may be sent and summed in bfloat16 or wider, within the bound.
A program may use at most 64 MiB of HBM per device.

```python
import math
import jax
import jax.numpy as jnp
from jax import lax

D = 4096
ATOM_DEV = 1024
ROWS = 128
ITERS = 3
BLOCK = 256
DEAD_MAX = 32
K = 16384
N_ATOMS = 16


def draw_dead_index(key, part):
    key = jax.random.fold_in(key, 11)
    keys = jax.random.split(key, N_ATOMS)
    picked = jax.vmap(lambda k: jax.random.permutation(k, BLOCK)[:DEAD_MAX])(keys)
    return picked.astype(jnp.int32)


def draw_dead_count(key, part):
    key = jax.random.fold_in(key, 12)
    first_key, second_key = jax.random.split(key)
    base = jax.random.randint(first_key, (N_ATOMS,), 0, DEAD_MAX // 2 + 1)
    chosen = jax.random.randint(second_key, (), 0, N_ATOMS)
    filled = jnp.where(jnp.arange(N_ATOMS) == chosen, DEAD_MAX, base)
    return filled.astype(jnp.int32)


def set_ends(entries, key, smallest, high):
    spot = [jax.random.randint(jax.random.fold_in(key, axis), (), 0, length) for axis, length in enumerate(entries.shape)]
    main_axis = entries.shape.index(max(entries.shape))
    next_to = spot[:main_axis] + [(spot[main_axis] + 1) % entries.shape[main_axis]] + spot[main_axis + 1:]
    return entries.at[tuple(spot)].set(smallest).at[tuple(next_to)].set(high)


def block_scale(rng, extent, cuts, smallest, top_value):
    gain, own = 1.0, jax.random.fold_in(rng, 6)
    for position, parts in cuts:
        heights = jnp.exp(jax.random.uniform(jax.random.fold_in(own, position), (parts,), jnp.float32, smallest / len(cuts), top_value / len(cuts)))
        gain = gain * jnp.repeat(heights, extent[position] // parts).reshape([-1 if axis == position else 1 for axis in range(len(extent))])
    return gain


def gaussian(stream_key, shape, deviation, most, cuts=(), kind=jnp.bfloat16):
    gain = block_scale(stream_key, shape, cuts, -0.22, 0.18) if cuts else 1.0
    drawn = jax.random.normal(stream_key, shape, jnp.float32) * deviation * gain
    return jnp.minimum(jnp.maximum(drawn, -most), most).astype(kind)


def setup_inputs(seed: int = 0, part: int = 0) -> dict:
    seeds = jax.random.split(jax.random.key(seed), 6)
    part_splits = jax.random.split(jax.random.fold_in(seeds[5], part), 6)
    xt = gaussian(part_splits[0], (D, ROWS), 1.0, 6.0)
    dictionary = gaussian(seeds[1], (K, D), D ** -0.5, 0.09375, ((0, 16),))
    dead_index = draw_dead_index(jax.random.fold_in(jax.random.fold_in(seeds[5], part), 71), part)
    dead_count = draw_dead_count(jax.random.fold_in(jax.random.fold_in(seeds[5], part), 71), part)
    refill_rows = set_ends(jax.random.randint(part_splits[4], (N_ATOMS, DEAD_MAX), 0, ROWS), jax.random.fold_in(part_splits[4], 1), 0, ROWS - 1).astype(jnp.int32)
    return {"xt": xt, "dictionary": dictionary, "dead_index": dead_index, "dead_count": dead_count, "refill_rows": refill_rows}


def reference(xt, dictionary, dead_index, dead_count, refill_rows):
    total_atoms = ATOM_DEV * N_ATOMS
    step_code = 1.0 / (1.0 + math.sqrt(total_atoms / D)) ** 2
    thresh = 0.8 * step_code
    step_dict = 2.0 / (math.sqrt(ROWS) * step_code * math.sqrt(D))
    shards = dictionary.reshape(N_ATOMS, ATOM_DEV, D)
    codes = jnp.zeros((ROWS, total_atoms), jnp.float32)
    xt_f = xt.astype(jnp.float32)
    res_b = xt
    codes_b = codes.astype(jnp.bfloat16)
    resid = xt_f
    for it in range(ITERS):
        res_now = res_b.astype(jnp.float32)

        def correlate(weights, res_now=res_now):
            return jnp.dot(weights.astype(jnp.float32), res_now, precision=lax.Precision.HIGHEST)
        corr = lax.map(correlate, shards)
        corr = jnp.transpose(corr, (2, 0, 1)).reshape(ROWS, total_atoms)
        moved = codes + step_code * corr
        codes = moved - jnp.clip(moved, -thresh, thresh)
        codes_b = codes.astype(jnp.bfloat16)
        code_shards = jnp.transpose(codes_b.reshape(ROWS, N_ATOMS, ATOM_DEV), (1, 2, 0))

        def accumulate(total, pair):
            weights, code_part = pair
            term = jnp.dot(weights.astype(jnp.float32).T, code_part.astype(jnp.float32), precision=lax.Precision.HIGHEST)
            return (total + term, None)
        recon, unused = lax.scan(accumulate, jnp.zeros((D, ROWS), xt_f.dtype), (shards, code_shards))
        resid = xt_f - recon
        res_b = resid.astype(jnp.bfloat16)
    block_codes = codes_b.reshape(ROWS, N_ATOMS, ATOM_DEV)[:, :, :BLOCK].astype(jnp.float32)
    res_f = res_b.astype(jnp.float32)
    grad = jnp.einsum('rnb,dr->nbd', block_codes, res_f, precision=lax.Precision.HIGHEST)
    updated = shards[:, :BLOCK].astype(jnp.float32) + step_dict * grad
    normed = updated * lax.rsqrt(lax.optimization_barrier(jnp.sum(updated * updated, axis=2, keepdims=True)) + 1e-06)
    valid = jnp.arange(DEAD_MAX, dtype=jnp.int32)[None, :] < dead_count[:, None]
    select = (refill_rows[:, :, None] == jnp.arange(ROWS, dtype=jnp.int32)[None, None, :]).astype(jnp.float32)
    cand = jnp.einsum('njr,dr->njd', select, res_f, precision=lax.Precision.HIGHEST)
    cand = cand * lax.rsqrt(lax.optimization_barrier(jnp.sum(cand * cand, axis=2, keepdims=True)) + 1e-06)
    place = ((dead_index[:, :, None] == jnp.arange(BLOCK, dtype=jnp.int32)[None, None, :]) & valid[:, :, None]).astype(jnp.float32)
    placed = jnp.einsum('njb,njd->nbd', place, cand, precision=lax.Precision.HIGHEST)
    hit = lax.optimization_barrier(jnp.sum(place, axis=1)) > 0.5
    new_block = jnp.where(hit[:, :, None], placed, normed).astype(jnp.bfloat16).reshape(N_ATOMS * BLOCK, D)
    return (codes_b, new_block, resid)
```

```python
import functools
import math

import jax
import jax.numpy as jnp
from jax import lax
from jax.experimental import pallas as pl
from jax.experimental.pallas import tpu as pltpu
from jax.sharding import PartitionSpec as P

ITERS = 3
BLOCK = 256
DEAD_MAX = 32
F32 = jnp.float32
BF16 = jnp.bfloat16


def consts(total_atoms, width, rows):
    step_code = 1.0 / (1.0 + math.sqrt(total_atoms / width)) ** 2
    thresh = 0.8 * step_code
    step_dict = 2.0 / (math.sqrt(rows) * step_code * math.sqrt(width))
    return step_code, thresh, step_dict


def kernel(n, consts, xt_ref, dict_ref, di_ref, dc_ref, rr_ref, codes_ref, nb_ref, res_ref,
           dic, z, acc, rb, csend, crecv, xsend, xrecv, zsend, zrecv, own, upd,
           dsem, cs, cr, xs, xr, zs, zr, gcs, gcr, gxs, gxr, gzs, gzr):
    step_code, thresh, step_dict = consts
    outer = n // 4
    share = xt_ref.shape[2]
    rows = xt_ref.shape[1]
    me = lax.axis_index("atoms")
    c = lax.rem(me, 2)
    i = lax.rem(me // 2, 2)
    o = me // 4

    def at(o_, i_, c_):
        return o_ * 4 + i_ * 2 + c_

    core_dev = at(o, i, 1 - c)
    x_dev = at(o, 1 - i, c)

    def turn(k):
        return lax.rem(o + k, outer)

    def rcopy(src, dst, ss, rs, dev):
        return pltpu.make_async_remote_copy(
            src_ref=src, dst_ref=dst, send_sem=ss, recv_sem=rs,
            device_id={"atoms": dev}, device_id_type=pl.DeviceIdType.MESH)

    def rs_core(o_, i_):
        s = o_ * 2 + i_
        return rcopy(csend.at[s], crecv.at[s], cs.at[s], cr.at[s], core_dev)

    def rs_x(o_):
        return rcopy(xsend.at[o_], xrecv.at[o_], xs.at[o_], xr.at[o_], x_dev)

    def rs_z(o_, slot):
        return rcopy(zsend.at[o_], zrecv.at[slot], zs.at[o_], zr.at[slot], at(o_, i, c))

    def ag_z(o_, slot):
        b = at(slot, i, c)
        return rcopy(rb.at[b], rb.at[b], gzs.at[o_], gzr.at[slot], at(o_, i, c))

    def ag_x(o_, i_):
        b = at(o_, i_, c)
        return rcopy(rb.at[b], rb.at[b], gxs.at[o_], gxr.at[o_], x_dev)

    def ag_core(o_, i_, c_):
        b = at(o_, i_, c_)
        s = o_ * 2 + i_
        return rcopy(rb.at[b], rb.at[b], gcs.at[s], gcr.at[s], core_dev)

    def load(b):
        return pltpu.make_async_copy(
            dict_ref.at[:, pl.ds(pl.multiple_of(b * share, share), share)], dic.at[b], dsem.at[b])

    def loop(count, body):
        lax.fori_loop(0, count, lambda k, u: (body(k), u)[1], 0)

    loop(n, lambda b: load(b).start())
    barrier = pltpu.get_barrier_semaphore()

    def greet(dev):
        pl.semaphore_signal(barrier, inc=1, device_id={"atoms": dev},
                            device_id_type=pl.DeviceIdType.MESH)

    greet(core_dev)
    greet(x_dev)
    loop(outer - 1, lambda k: greet(at(turn(k + 1), i, c)))

    def corr(src, b):
        acc[...] += lax.dot_general(src[b], dic[b], (((1,), (1,)), ((), ())),
                                    preferred_element_type=F32)

    def term(b):
        return jnp.dot(codes_ref[...], dic[b], preferred_element_type=F32)

    place = (di_ref[...] == lax.broadcasted_iota(jnp.int32, (BLOCK, DEAD_MAX), 0)) & (
        lax.broadcasted_iota(jnp.int32, (BLOCK, DEAD_MAX), 1) < dc_ref[...])
    place = jnp.where(place, 1.0, 0.0).astype(F32)
    hit = jnp.sum(place, axis=1, keepdims=True) > 0.5
    pick = jnp.where(rr_ref[...] == lax.broadcasted_iota(jnp.int32, (rows, DEAD_MAX), 0), 1.0, 0.0)
    onehot = lax.dot_general(place.astype(BF16), pick.astype(BF16), (((1,), (1,)), ((), ())),
                             preferred_element_type=F32)

    acc[...] = jnp.zeros_like(acc)

    def first(b):
        load(b).wait()
        corr(xt_ref, b)

    loop(n, first)
    pl.semaphore_wait(barrier, outer + 1)

    for it in range(ITERS):
        moved = step_code * acc[...] if it == 0 else z[...] + step_code * acc[...]
        zn = moved - jnp.clip(moved, -thresh, thresh)
        codes_ref[...] = zn.astype(BF16)
        if it < ITERS - 1:
            z[...] = zn
            acc[...] = jnp.zeros_like(acc)
        else:
            mix = jnp.where(hit, onehot, zn[:, :BLOCK].T).astype(BF16)
            sq = [jnp.zeros((BLOCK, 1), F32)]

        def to_core(i_):
            def body(k):
                o_ = turn(k)
                csend[o_ * 2 + i_] = term(at(o_, i_, 1 - c)).astype(BF16)
                rs_core(o_, i_).start()
            return body

        def to_x(k):
            o_ = turn(k)
            part = term(at(o_, 1 - i, c))
            rs_core(o_, 1 - i).wait_recv()
            xsend[o_] = (part + crecv[o_ * 2 + 1 - i].astype(F32)).astype(BF16)
            rs_x(o_).start()

        def chip_sum(o_):
            part = term(at(o_, i, c))
            rs_core(o_, i).wait_recv()
            part += crecv[o_ * 2 + i].astype(F32)
            rs_x(o_).wait_recv()
            return part + xrecv[o_].astype(F32)

        def to_z(k):
            o_ = turn(k + 1)
            zsend[o_] = chip_sum(o_).astype(BF16)
            rs_z(o_, o).start()

        def from_z(k):
            o_ = turn(k + 1)
            rs_z(o_, o_).wait_recv()
            own[...] += zrecv[o_].astype(F32)

        loop(outer, lambda k: to_core(1 - i)(k + 1))
        loop(outer, lambda k: to_x(k + 1))
        loop(outer, lambda k: to_core(i)(k + 1))
        loop(outer - 1, to_z)
        own[...] = chip_sum(o)
        loop(outer - 1, from_z)
        resid = xt_ref[me].astype(F32) - own[...]
        rb[me] = resid.astype(BF16)
        if it == ITERS - 1:
            res_ref[...] = resid.T

        if it < ITERS - 1:
            def use(b):
                corr(rb, b)
        else:
            def use(b):
                g = jnp.dot(mix, rb[b], preferred_element_type=F32)
                u = jnp.where(hit, g, dic[b, :BLOCK].astype(F32) + step_dict * g)
                upd[b] = u

        loop(outer - 1, lambda k: ag_z(turn(k + 1), o).start())
        ag_x(o, i).start()
        ag_core(o, i, c).start()
        use(me)

        def got_z(k):
            o_ = turn(k + 1)
            ag_z(o_, o_).wait_recv()
            ag_x(o_, i).start()
            ag_core(o_, i, c).start()
            use(at(o_, i, c))

        def got_x(k):
            o_ = turn(k)
            ag_x(o_, 1 - i).wait_recv()
            ag_core(o_, 1 - i, c).start()
            use(at(o_, 1 - i, c))

        def got_core(i_):
            def body(k):
                o_ = turn(k)
                ag_core(o_, i_, 1 - c).wait_recv()
                use(at(o_, i_, 1 - c))
            return body

        loop(outer - 1, got_z)
        loop(outer, got_x)
        loop(outer, got_core(i))
        loop(outer, got_core(1 - i))

        def sent(k):
            o_ = turn(k)
            for i_ in (i, 1 - i):
                rs_core(o_, i_).wait_send()
                ag_core(o_, i_, c).wait_send()
            rs_x(o_).wait_send()
            ag_x(o_, i).wait_send()

        def sent_z(k):
            o_ = turn(k + 1)
            rs_z(o_, o).wait_send()
            ag_z(o_, o).wait_send()

        loop(outer, sent)
        loop(outer - 1, sent_z)

    total = jnp.zeros((BLOCK, share), F32)
    total = lax.fori_loop(0, n, lambda b, t: t + upd[b] * upd[b], total)
    scale = lax.rsqrt(jnp.sum(total, axis=1, keepdims=True) + 1e-06)
    for b in range(n):
        nb_ref[:, b * share:(b + 1) * share] = (upd[b] * scale).astype(BF16)


def fused(xt, dictionary, dead_index, dead_count, refill_rows):
    n = lax.axis_size("atoms")
    local_atoms, width = dictionary.shape
    rows = xt.shape[1]
    share = width // n
    outer = n // 4
    x_blocks = xt.reshape(n, share, rows).transpose(0, 2, 1)
    vmem = pl.BlockSpec(memory_space=pltpu.VMEM)
    dma = pltpu.SemaphoreType.DMA
    part = (rows, share)
    codes, block, resid = pl.pallas_call(
        functools.partial(kernel, n, consts(local_atoms * n, width, rows)),
        out_shape=(
            jax.ShapeDtypeStruct((rows, local_atoms), BF16),
            jax.ShapeDtypeStruct((BLOCK, width), BF16),
            jax.ShapeDtypeStruct((share, rows), F32),
        ),
        in_specs=[vmem, pl.BlockSpec(memory_space=pl.ANY), vmem, vmem, vmem],
        out_specs=(vmem, vmem, vmem),
        scratch_shapes=[
            pltpu.VMEM((n, local_atoms, share), BF16),
            pltpu.VMEM((rows, local_atoms), F32),
            pltpu.VMEM((rows, local_atoms), F32),
            pltpu.VMEM((n,) + part, BF16),
            pltpu.VMEM((n // 2,) + part, BF16),
            pltpu.VMEM((n // 2,) + part, BF16),
            pltpu.VMEM((outer,) + part, BF16),
            pltpu.VMEM((outer,) + part, BF16),
            pltpu.VMEM((outer,) + part, BF16),
            pltpu.VMEM((outer,) + part, BF16),
            pltpu.VMEM(part, F32),
            pltpu.VMEM((n, BLOCK, share), F32),
            dma((n,)),
            dma((n // 2,)), dma((n // 2,)),
            dma((outer,)), dma((outer,)), dma((outer,)), dma((outer,)),
            dma((n // 2,)), dma((n // 2,)),
            dma((outer,)), dma((outer,)), dma((outer,)), dma((outer,)),
        ],
        compiler_params=pltpu.CompilerParams(
            collective_id=0, has_side_effects=True, vmem_limit_bytes=48 * 2**20),
    )(x_blocks, dictionary, dead_index, dead_count.reshape(1, 1), refill_rows)
    return codes, block, resid


def plain(xt, dictionary, dead_index, dead_count, refill_rows):
    count_atoms = lax.axis_size("atoms")
    local_atoms, width = dictionary.shape
    rows = xt.shape[1]
    step_code, thresh, step_dict = consts(local_atoms * count_atoms, width, rows)
    share = width // count_atoms
    first = lax.axis_index("atoms") * share
    codes = jnp.zeros((rows, local_atoms), F32)
    res_b = xt
    for step in range(ITERS):
        corr = jnp.dot(dictionary, res_b, preferred_element_type=F32).T
        moved = codes + step_code * corr
        codes = moved - jnp.clip(moved, -thresh, thresh)
        codes_b = codes.astype(BF16)
        term = jnp.dot(codes_b, dictionary, preferred_element_type=F32).T
        resid_full = xt.astype(F32) - lax.psum(term, "atoms")
        res_b = resid_full.astype(BF16)
    resid_share = lax.dynamic_slice_in_dim(resid_full, first, share, 0)
    grad = jnp.dot(res_b, codes_b[:, :BLOCK], preferred_element_type=F32).T
    updated = dictionary[:BLOCK].astype(F32) + step_dict * grad
    valid = jnp.arange(DEAD_MAX, dtype=jnp.int32) < dead_count[0]
    place = (dead_index[0][None, :] == jnp.arange(BLOCK, dtype=jnp.int32)[:, None]) & valid[None, :]
    pick = refill_rows[0][:, None] == jnp.arange(rows, dtype=jnp.int32)[None, :]
    onehot = jnp.dot(place.astype(BF16), pick.astype(BF16), preferred_element_type=F32)
    cand = jnp.dot(onehot.astype(BF16), res_b.T, preferred_element_type=F32)
    mixed = jnp.where(jnp.any(place, axis=1)[:, None], cand, updated)
    new_block = mixed * lax.rsqrt(jnp.sum(mixed * mixed, axis=1, keepdims=True) + 1e-06)
    return codes_b, new_block.astype(BF16), resid_share


def shards(xt, dictionary, *rest):
    n = lax.axis_size("atoms")
    fits = n % 4 == 0 and n >= 8 and xt.shape[0] % (n * 128) == 0
    return (fused if fits else plain)(xt, dictionary, *rest)


def solution(mesh):
    placed = (
        P(None, "groups"),
        P("atoms", None),
        P(("groups", "atoms"), None),
        P(("groups", "atoms")),
        P(("groups", "atoms"), None),
    )
    return jax.shard_map(
        shards,
        mesh=mesh,
        in_specs=placed,
        out_specs=(P("groups", "atoms"), P(("groups", "atoms"), None), P("atoms", "groups")),
        check_vma=False,
    )
```

```python
import functools
import math

import jax
import jax.numpy as jnp
from jax import lax
from jax.experimental import pallas as pl
from jax.experimental.pallas import tpu as pltpu
from jax.sharding import PartitionSpec as P

ITERS = 3
BLOCK = 256
DEAD_MAX = 32
HALVES = 2
F32 = jnp.float32
BF16 = jnp.bfloat16


def consts(total_atoms, width, rows):
    step_code = 1.0 / (1.0 + math.sqrt(total_atoms / width)) ** 2
    thresh = 0.8 * step_code
    step_dict = 2.0 / (math.sqrt(rows) * step_code * math.sqrt(width))
    return step_code, thresh, step_dict


def kernel(n, consts, xt_ref, dict_ref, di_ref, dc_ref, rr_ref, codes_ref, nb_ref, res_ref,
           dic, z, acc, xb, rb, csend, crecv, xsend, xrecv, zsend, zrecv, own, upd,
           dsem, cs, cr, xs, xr, zs, zr, gcs, gcr, gxs, gxr, gzs, gzr):
    step_code, thresh, step_dict = consts
    outer = n // 4
    rows = xt_ref.shape[1]
    share = xt_ref.shape[0] // n
    piece = rows // HALVES
    me = lax.axis_index("atoms")
    c = lax.rem(me, 2)
    i = lax.rem(me // 2, 2)
    o = me // 4

    def at(o_, i_, c_):
        return o_ * 4 + i_ * 2 + c_

    core_dev = at(o, i, 1 - c)
    x_dev = at(o, 1 - i, c)

    def turn(k):
        return lax.rem(o + k, outer)

    def rcopy(src, dst, ss, rs, dev):
        return pltpu.make_async_remote_copy(
            src_ref=src, dst_ref=dst, send_sem=ss, recv_sem=rs,
            device_id={"atoms": dev}, device_id_type=pl.DeviceIdType.MESH)

    def cut(h):
        return pl.ds(h * piece, piece)

    def rs_core(o_, i_, h):
        s = o_ * 2 + i_
        return rcopy(csend.at[s, cut(h)], crecv.at[s, cut(h)], cs.at[h, s], cr.at[h, s], core_dev)

    def rs_x(o_, h):
        return rcopy(xsend.at[o_, cut(h)], xrecv.at[o_, cut(h)], xs.at[h, o_], xr.at[h, o_], x_dev)

    def rs_z(o_, slot, h):
        return rcopy(zsend.at[o_, cut(h)], zrecv.at[slot, cut(h)], zs.at[h, o_], zr.at[h, slot],
                     at(o_, i, c))

    def ag_z(o_, slot, h):
        b = rb.at[at(slot, i, c), cut(h)]
        return rcopy(b, b, gzs.at[h, o_], gzr.at[h, slot], at(o_, i, c))

    def ag_x(o_, i_, h):
        b = rb.at[at(o_, i_, c), cut(h)]
        return rcopy(b, b, gxs.at[h, o_], gxr.at[h, o_], x_dev)

    def ag_core(o_, i_, c_, h):
        b = rb.at[at(o_, i_, c_), cut(h)]
        s = o_ * 2 + i_
        return rcopy(b, b, gcs.at[h, s], gcr.at[h, s], core_dev)

    def load(b):
        return pltpu.make_async_copy(
            dict_ref.at[:, pl.ds(pl.multiple_of(b * share, share), share)], dic.at[b], dsem.at[b])

    def loop(count, body):
        lax.fori_loop(0, count, lambda k, u: (body(k), u)[1], 0)

    loop(n, lambda b: load(b).start())
    barrier = pltpu.get_barrier_semaphore()

    def greet(dev):
        pl.semaphore_signal(barrier, inc=1, device_id={"atoms": dev},
                            device_id_type=pl.DeviceIdType.MESH)

    greet(core_dev)
    greet(x_dev)
    loop(outer - 1, lambda k: greet(at(turn(k + 1), i, c)))

    def corr(src, b):
        acc[...] += lax.dot_general(src[b], dic[b], (((1,), (1,)), ((), ())),
                                    preferred_element_type=F32)

    def term(b):
        return jnp.dot(codes_ref[...], dic[b], preferred_element_type=F32)

    place = (di_ref[...] == lax.broadcasted_iota(jnp.int32, (BLOCK, DEAD_MAX), 0)) & (
        lax.broadcasted_iota(jnp.int32, (BLOCK, DEAD_MAX), 1) < dc_ref[...])
    place = jnp.where(place, 1.0, 0.0).astype(F32)
    hit = jnp.sum(place, axis=1, keepdims=True) > 0.5
    pick = jnp.where(rr_ref[...] == lax.broadcasted_iota(jnp.int32, (rows, DEAD_MAX), 0), 1.0, 0.0)
    onehot = lax.dot_general(place.astype(BF16), pick.astype(BF16), (((1,), (1,)), ((), ())),
                             preferred_element_type=F32)

    acc[...] = jnp.zeros_like(acc)

    def first(b):
        first_row = pl.multiple_of(b * share, share)
        xb[b] = xt_ref[pl.ds(first_row, share), :].T
        load(b).wait()
        corr(xb, b)

    loop(n, first)
    pl.semaphore_wait(barrier, outer + 1)

    def each(count, body):
        def both(k):
            for h in range(HALVES):
                body(k, h)
        loop(count, both)

    def reduced():
        each(n // 2, lambda s, h: rs_core(s // 2, lax.rem(s, 2), h).wait_send())
        each(outer, lambda o_, h: rs_x(o_, h).wait_send())
        each(outer - 1, lambda k, h: rs_z(turn(k + 1), o, h).wait_send())

    def gathered():
        each(n // 2, lambda s, h: ag_core(s // 2, lax.rem(s, 2), c, h).wait_send())
        each(outer, lambda o_, h: ag_x(o_, i, h).wait_send())
        each(outer - 1, lambda k, h: ag_z(turn(k + 1), o, h).wait_send())

    for it in range(ITERS):
        moved = step_code * acc[...] if it == 0 else z[...] + step_code * acc[...]
        zn = moved - jnp.clip(moved, -thresh, thresh)
        codes_ref[...] = zn.astype(BF16)
        if it < ITERS - 1:
            z[...] = zn
            acc[...] = jnp.zeros_like(acc)
        else:
            mix = jnp.where(hit, onehot, zn[:, :BLOCK].T).astype(BF16)
            sq = [jnp.zeros((BLOCK, 1), F32)]

        def to_core(i_):
            def body(k):
                o_ = turn(k)
                csend[o_ * 2 + i_] = term(at(o_, i_, 1 - c)).astype(BF16)
                for h in range(HALVES):
                    rs_core(o_, i_, h).start()
            return body

        def to_x(k):
            o_ = turn(k)
            own[...] = term(at(o_, 1 - i, c))
            for h in range(HALVES):
                rs_core(o_, 1 - i, h).wait_recv()
                both = own[cut(h)] + crecv[o_ * 2 + 1 - i, cut(h)].astype(F32)
                xsend[o_, cut(h)] = both.astype(BF16)
                rs_x(o_, h).start()

        def chip_sum(o_, h):
            rs_core(o_, i, h).wait_recv()
            both = own[cut(h)] + crecv[o_ * 2 + i, cut(h)].astype(F32)
            rs_x(o_, h).wait_recv()
            return both + xrecv[o_, cut(h)].astype(F32)

        def to_z(k):
            o_ = turn(k + 1)
            own[...] = term(at(o_, i, c))
            for h in range(HALVES):
                zsend[o_, cut(h)] = chip_sum(o_, h).astype(BF16)
                rs_z(o_, o, h).start()

        loop(outer, lambda k: to_core(1 - i)(k + 1))
        if it > 0:
            gathered()
        loop(outer, lambda k: to_x(k + 1))
        loop(outer, lambda k: to_core(i)(k + 1))
        loop(outer - 1, to_z)
        own[...] = term(me)
        for h in range(HALVES):
            own[cut(h)] = chip_sum(o, h)

        for h in range(HALVES):
            def from_z(k, h=h):
                o_ = turn(k + 1)
                rs_z(o_, o_, h).wait_recv()
                own[cut(h)] += zrecv[o_, cut(h)].astype(F32)

            loop(outer - 1, from_z)
            resid = xb[me, cut(h)].astype(F32) - own[cut(h)]
            own[cut(h)] = resid
            rb[me, cut(h)] = resid.astype(BF16)
            loop(outer - 1, lambda k, h=h: ag_z(turn(k + 1), o, h).start())
            ag_x(o, i, h).start()
            ag_core(o, i, c, h).start()
        if it == ITERS - 1:
            res_ref[...] = own[...].T

        if it < ITERS - 1:
            def use(b):
                corr(rb, b)
        else:
            def use(b):
                g = jnp.dot(mix, rb[b], preferred_element_type=F32)
                u = jnp.where(hit, g, dic[b, :BLOCK].astype(F32) + step_dict * g)
                upd[b] = u

        use(me)
        reduced()

        def got_z(h):
            def body(k):
                o_ = turn(k + 1)
                ag_z(o_, o_, h).wait_recv()
                ag_x(o_, i, h).start()
                ag_core(o_, i, c, h).start()
                if h == HALVES - 1:
                    use(at(o_, i, c))
            return body

        def got_x(k):
            o_ = turn(k)
            for h in range(HALVES):
                ag_x(o_, 1 - i, h).wait_recv()
                ag_core(o_, 1 - i, c, h).start()
            use(at(o_, 1 - i, c))

        def got_core(i_):
            def body(k):
                o_ = turn(k)
                for h in range(HALVES):
                    ag_core(o_, i_, 1 - c, h).wait_recv()
                use(at(o_, i_, 1 - c))
            return body

        for h in range(HALVES):
            loop(outer - 1, got_z(h))
        loop(outer, got_x)
        loop(outer, got_core(i))
        loop(outer, got_core(1 - i))

    gathered()
    total = jnp.zeros((BLOCK, share), F32)
    total = lax.fori_loop(0, n, lambda b, t: t + upd[b] * upd[b], total)
    scale = lax.rsqrt(jnp.sum(total, axis=1, keepdims=True) + 1e-06)
    for b in range(n):
        nb_ref[:, b * share:(b + 1) * share] = (upd[b] * scale).astype(BF16)


def fused(xt, dictionary, dead_index, dead_count, refill_rows):
    n = lax.axis_size("atoms")
    local_atoms, width = dictionary.shape
    rows = xt.shape[1]
    share = width // n
    outer = n // 4
    vmem = pl.BlockSpec(memory_space=pltpu.VMEM)
    dma = pltpu.SemaphoreType.DMA
    part = (rows, share)
    codes, block, resid = pl.pallas_call(
        functools.partial(kernel, n, consts(local_atoms * n, width, rows)),
        out_shape=(
            jax.ShapeDtypeStruct((rows, local_atoms), BF16),
            jax.ShapeDtypeStruct((BLOCK, width), BF16),
            jax.ShapeDtypeStruct((share, rows), F32),
        ),
        in_specs=[vmem, pl.BlockSpec(memory_space=pl.ANY), vmem, vmem, vmem],
        out_specs=(vmem, vmem, vmem),
        scratch_shapes=[
            pltpu.VMEM((n, local_atoms, share), BF16),
            pltpu.VMEM((rows, local_atoms), F32),
            pltpu.VMEM((rows, local_atoms), F32),
            pltpu.VMEM((n,) + part, BF16),
            pltpu.VMEM((n,) + part, BF16),
            pltpu.VMEM((n // 2,) + part, BF16),
            pltpu.VMEM((n // 2,) + part, BF16),
            pltpu.VMEM((outer,) + part, BF16),
            pltpu.VMEM((outer,) + part, BF16),
            pltpu.VMEM((outer,) + part, BF16),
            pltpu.VMEM((outer,) + part, BF16),
            pltpu.VMEM(part, F32),
            pltpu.VMEM((n, BLOCK, share), F32),
            dma((n,)),
            dma((HALVES, n // 2)), dma((HALVES, n // 2)),
            dma((HALVES, outer)), dma((HALVES, outer)), dma((HALVES, outer)), dma((HALVES, outer)),
            dma((HALVES, n // 2)), dma((HALVES, n // 2)),
            dma((HALVES, outer)), dma((HALVES, outer)), dma((HALVES, outer)), dma((HALVES, outer)),
        ],
        compiler_params=pltpu.CompilerParams(
            collective_id=0, has_side_effects=True, vmem_limit_bytes=48 * 2**20),
    )(xt, dictionary, dead_index, dead_count.reshape(1, 1), refill_rows)
    return codes, block, resid


def plain(xt, dictionary, dead_index, dead_count, refill_rows):
    count_atoms = lax.axis_size("atoms")
    local_atoms, width = dictionary.shape
    rows = xt.shape[1]
    step_code, thresh, step_dict = consts(local_atoms * count_atoms, width, rows)
    share = width // count_atoms
    first = lax.axis_index("atoms") * share
    codes = jnp.zeros((rows, local_atoms), F32)
    res_b = xt
    for step in range(ITERS):
        corr = jnp.dot(dictionary, res_b, preferred_element_type=F32).T
        moved = codes + step_code * corr
        codes = moved - jnp.clip(moved, -thresh, thresh)
        codes_b = codes.astype(BF16)
        term = jnp.dot(codes_b, dictionary, preferred_element_type=F32).T
        resid_full = xt.astype(F32) - lax.psum(term, "atoms")
        res_b = resid_full.astype(BF16)
    resid_share = lax.dynamic_slice_in_dim(resid_full, first, share, 0)
    grad = jnp.dot(res_b, codes_b[:, :BLOCK], preferred_element_type=F32).T
    updated = dictionary[:BLOCK].astype(F32) + step_dict * grad
    valid = jnp.arange(DEAD_MAX, dtype=jnp.int32) < dead_count[0]
    place = (dead_index[0][None, :] == jnp.arange(BLOCK, dtype=jnp.int32)[:, None]) & valid[None, :]
    pick = refill_rows[0][:, None] == jnp.arange(rows, dtype=jnp.int32)[None, :]
    onehot = jnp.dot(place.astype(BF16), pick.astype(BF16), preferred_element_type=F32)
    cand = jnp.dot(onehot.astype(BF16), res_b.T, preferred_element_type=F32)
    mixed = jnp.where(jnp.any(place, axis=1)[:, None], cand, updated)
    new_block = mixed * lax.rsqrt(jnp.sum(mixed * mixed, axis=1, keepdims=True) + 1e-06)
    return codes_b, new_block.astype(BF16), resid_share


def shards(xt, dictionary, *rest):
    n = lax.axis_size("atoms")
    fits = n % 4 == 0 and n >= 8 and xt.shape[0] % (n * 128) == 0
    return (fused if fits else plain)(xt, dictionary, *rest)


def solution(mesh):
    placed = (
        P(None, "groups"),
        P("atoms", None),
        P(("groups", "atoms"), None),
        P(("groups", "atoms")),
        P(("groups", "atoms"), None),
    )
    return jax.shard_map(
        shards,
        mesh=mesh,
        in_specs=placed,
        out_specs=(P("groups", "atoms"), P(("groups", "atoms"), None), P("atoms", "groups")),
        check_vma=False,
    )
```
